32 devices in a mesh: groups: 2 (over x), expert: 16 (over z, y, core), dp: 1.
Axes of the slice: x: 2, y: 2, z: 4, core: 2. Of those that a mesh axis runs over, the one named last changes fastest.
Arguments:
- latent_pool: bfloat16 [256, 36864], P(('groups', 'expert')), parts along dimension 0, may hold values from -6 to 6
- page_owner: int32 [64, 8], P(('groups', 'expert')), parts along dimension 0, may hold values from 0 to 15, all different within a row; in each aligned block of 2 rows (0 to 1, 2 to 3, ...) at most 2 rows name the same one
- page_slot: int32 [64, 8], P(('groups', 'expert')), parts along dimension 0, may hold values from 0 to 7
- prefix_len: int32 [64], P(('groups', 'expert')), parts along dimension 0, may hold values from 449 to 512
- queries: bfloat16 [64, 32, 36864], P(('groups', 'expert'), None, 'dp'), parts along dimension 0, may hold values from -30 to 30
- new_latent: bfloat16 [64, 18432], P(('groups', 'expert')), parts along dimension 0, may hold values from -5 to 5
- tokens: bfloat16 [2048, 3584], P(('groups', 'expert', 'dp')), parts along dimension 0, may hold values from -6 to 6
- expert_ids: int32 [2048, 4], P(('groups', 'expert', 'dp')), parts along dimension 0, may hold values from 0 to 15, all different within a row; in each aligned block of 64 rows (0 to 63, 64 to 127, ...) at most 24 rows name the same one
- gates: float32 [2048, 4], P(('groups', 'expert', 'dp')), parts along dimension 0, may hold values from 0.2 to 1
- w_gate: bfloat16 [16, 3584, 1024], P(('expert', 'dp')), may hold values from -0.09375 to 0.09375
- w_up: bfloat16 [16, 3584, 1024], P(('expert', 'dp')), may hold values from -0.09375 to 0.09375
- w_down: bfloat16 [16, 1024, 3584], P(('expert', 'dp')), may hold values from -0.1875 to 0.1875
Outputs:
- context: bfloat16 [64, 32, 32768], P(('groups', 'expert'), None, 'dp'), parts along dimension 0
- moe_out: bfloat16 [2048, 3584], P(('groups', 'expert', 'dp')), parts along dimension 0
The draws below stay inside these ranges and needn't reach their ends.
There are 2 independent parts, one for each index of `groups`. The reference program is written for one: setup_inputs(seed, part) draws one part's arguments, and reference() takes and returns one part's arrays. A program takes and returns all parts, laid end to end along the dimension named above; an argument that names none is the same for every part. Nothing has to cross between parts.
Inputs may be any that keep to these rules, and one draw needn't show every extreme that they name: `page_owner`: each row names 8 different owners; within the 2 rows of one device no owner is named more than 2 times, and in some such block one owner is named exactly 2 times. `expert_ids`: each row names 4 different experts; within the 64 rows of one device no expert is named more than 24 times, and in some such block one expert is named exactly 24 times.
All inputs are finite; a program needn't handle non-finite values.
Results may differ from the reference program's by a relative error of at most 0.0057.
Values may be sent and summed in bfloat16 or wider, within the bound.
A program may use at most 128 MiB of HBM per device.

```python
import math
import jax
import jax.numpy as jnp
import numpy as np
from jax import lax

D = 3584
FF = 1024
H = 64
LATENT = 512
LAT = 576
PAGE = 64
MAXP = 8
NEW = 32
REQ_DEV = 2
EXPERTS = 16
TOP = 4
CAPP = 2
POOL_DEV = 8
OWNERS = 16
REQUESTS = 32
TOKENS = 1024
TOK_DEV = 64
SLICES = 16
SPLIT = 1
FF_SLICE = 1024
CAP = 24


def shared_latent(key):
    return jnp.clip(jax.random.normal(key, (REQUESTS, NEW, LAT), jnp.float32), -5.0, 5.0)


def draw_new_latent(key, part):
    latent = shared_latent(key)
    return latent.reshape(REQUESTS, NEW * LAT).astype(jnp.bfloat16)


def draw_queries(key, part):
    key = jax.random.fold_in(key, 5)
    key_values = jax.random.fold_in(key, 0)
    values = jnp.clip(jax.random.normal(key_values, (REQUESTS, NEW, H, LAT), jnp.float32), -5.0, 5.0)
    return values.reshape(REQUESTS, NEW, H * LAT).astype(jnp.bfloat16)


def set_ends(result, rng, low, largest):
    longest = result.shape.index(max(result.shape))
    spots = []
    for shift in (0, 1):
        where = [jax.random.randint(jax.random.fold_in(rng, axis), (), 0, length) for axis, length in enumerate(result.shape)]
        where[longest] = (where[longest] + shift) % result.shape[longest]
        spots.append(tuple(where))
    return result.at[spots[0]].set(low).at[spots[1]].set(largest)


def levels(stream_key, dims, cuts, smallest, largest):
    factor_of = 1.0
    for axis_at, blocks in cuts:
        heights = jax.random.uniform(jax.random.fold_in(jax.random.fold_in(stream_key, 6), axis_at), (blocks,), jnp.float32, smallest / len(cuts), largest / len(cuts))
        factor_of = factor_of * jnp.repeat(jnp.exp(heights), dims[axis_at] // blocks).reshape((-1,) + (1,) * (len(dims) - 1 - axis_at))
    return factor_of


def deal_out(key, own, number, rows, number_of, top, most, lean):
    order = jax.random.permutation(key, number_of)
    crowded, common = shares(number_of, rows * top, most, lean, True), shares(number_of, rows * top, most, lean, False)
    places = jnp.arange(number_of)

    def named(tallies, offset_by):
        used = int((tallies > 0).sum())
        fixed = max(1, used // 4)
        moved = fixed + (places - fixed + offset_by * (used - fixed)) % max(1, number_of - fixed)
        return jnp.zeros((number_of,), jnp.int32).at[order[jnp.where(places < fixed, places, moved)]].set(jnp.asarray(tallies, jnp.int32))

    tallies = jnp.where(number % 4 == 0, named(crowded, number // 4), named(common, number - number // 4 - 1))
    mixed = jax.random.permutation(jax.random.fold_in(own, 3), number_of)
    source_of, sink = mixed[0:number_of // 2 * 2:2], mixed[1:number_of // 2 * 2:2]
    room = jnp.minimum(tallies[source_of] - 1, most - tallies[sink]) // 2
    room = jnp.where((source_of == order[0]) | (sink == order[0]) | (tallies[sink] == 0), 0, jnp.maximum(room, 0))
    moved = jax.random.randint(jax.random.fold_in(own, 4), (number_of // 2,), 0, 1 << 20) % (room + 1)
    tallies = tallies.at[source_of].add(-moved).at[sink].add(moved)
    items = jnp.searchsorted(jnp.cumsum(tallies), jnp.arange(rows * top), side="right").astype(jnp.int32)
    table = items.reshape(top, rows).T
    table = table[jax.random.permutation(jax.random.fold_in(own, 1), rows)]
    offset_by = jax.random.randint(jax.random.fold_in(own, 2), (rows, 1), 0, top)
    return jnp.take_along_axis(table, (jnp.arange(top)[None, :] + offset_by) % top, axis=1)


def shares(count, total, bound, slope, full):
    portions = [(1 << 20) // math.isqrt(standing ** slope) + 1 for standing in range(1, count + 1)]
    largest = bound if full else min(bound, max(-(-total // count), total * portions[0] // sum(portions)))
    least = 1 if total - largest >= count - 1 else 0
    holding, rest = [largest] + [least] * (count - 1), total - largest - least * (count - 1)
    while rest > 0:
        movable = [i for i in range(1, count) if holding[i] < largest] or [i for i in range(1, count) if holding[i] < bound]
        whole, left = sum([portions[i] for i in movable]), rest
        for i in movable:
            addition = min(bound - holding[i], max(1, left * portions[i] // whole), rest)
            holding[i] = holding[i] + addition
            rest = rest - addition
    return np.array(holding)


def bell_draw(stream_key, extent, deviation, reach, shards=(), kind=jnp.bfloat16):
    gain = levels(stream_key, extent, shards, -0.22, 0.18) if shards else 1.0
    array = jax.random.normal(stream_key, extent, jnp.float32) * deviation * gain
    return jnp.minimum(jnp.maximum(array, -reach), reach).astype(kind)


def setup_inputs(seed: int = 0, part: int = 0) -> dict:
    seeds = jax.random.split(jax.random.key(seed), 13)
    own_keys = jax.random.split(jax.random.fold_in(seeds[12], part), 13)
    latent_pool = bell_draw(own_keys[0], (OWNERS * POOL_DEV, PAGE * LAT), 1.0, 6.0, ((0, 16),))
    page_owner_keys = jax.random.split(jax.random.fold_in(own_keys[1], 1), REQUESTS // REQ_DEV)
    page_owner_turns = jax.random.permutation(jax.random.fold_in(own_keys[1], 3), REQUESTS // REQ_DEV)
    page_owner = jax.vmap(lambda own, number: deal_out(jax.random.fold_in(own_keys[1], 2), own, number, REQ_DEV, OWNERS, MAXP, CAPP, 2))(page_owner_keys, page_owner_turns).reshape((REQUESTS, MAXP))
    page_slot = set_ends(jax.random.randint(own_keys[2], (REQUESTS, MAXP), 0, POOL_DEV), jax.random.fold_in(own_keys[2], 1), 0, POOL_DEV - 1).astype(jnp.int32)
    prefix_len = set_ends(jax.random.randint(own_keys[3], (REQUESTS,), (MAXP - 1) * PAGE + 1, MAXP * PAGE + 1), jax.random.fold_in(own_keys[3], 1), (MAXP - 1) * PAGE + 1, MAXP * PAGE).astype(jnp.int32)
    queries = draw_queries(jax.random.fold_in(jax.random.fold_in(seeds[12], part), 71), part)
    new_latent = draw_new_latent(jax.random.fold_in(jax.random.fold_in(seeds[12], part), 71), part)
    tokens = bell_draw(own_keys[6], (TOKENS, D), 1.0, 6.0, ((0, 16),))
    expert_ids_keys = jax.random.split(jax.random.fold_in(own_keys[7], 1), TOKENS // TOK_DEV)
    expert_ids_turns = jax.random.permutation(jax.random.fold_in(own_keys[7], 3), TOKENS // TOK_DEV)
    expert_ids = jax.vmap(lambda own, number: deal_out(jax.random.fold_in(own_keys[7], 2), own, number, TOK_DEV, EXPERTS, TOP, CAP, 2))(expert_ids_keys, expert_ids_turns).reshape((TOKENS, TOP))
    gates = jnp.clip(0.2 + 0.8 * jax.random.uniform(own_keys[8], (TOKENS, TOP), jnp.float32) ** levels(own_keys[8], (TOKENS, TOP), ((0, 16),), -0.2, 0.2), 0.2, 1.0)
    w_gate = bell_draw(seeds[9], (SLICES, D, FF_SLICE), D ** -0.5, 0.09375, ((0, 16),))
    w_up = bell_draw(seeds[10], (SLICES, D, FF_SLICE), D ** -0.5, 0.09375, ((0, 16),))
    w_down = bell_draw(seeds[11], (SLICES, FF_SLICE, D), FF ** -0.5, 0.1875, ((0, 16),))
    return {"latent_pool": latent_pool, "page_owner": page_owner, "page_slot": page_slot, "prefix_len": prefix_len, "queries": queries, "new_latent": new_latent, "tokens": tokens, "expert_ids": expert_ids, "gates": gates, "w_gate": w_gate, "w_up": w_up, "w_down": w_down}


score_scale = 192.0 ** -0.5


def attend(packed):
    query_rows, keys_all, length = packed
    query_heads = query_rows.astype(jnp.float32).reshape(NEW, H, LAT)
    keys_f = keys_all.astype(jnp.float32)
    scores = jnp.einsum("nhl,kl->hnk", query_heads, keys_f) * score_scale
    prefix_cap = MAXP * PAGE
    position = jnp.arange(prefix_cap + NEW, dtype=jnp.int32)
    row_index = jnp.arange(NEW, dtype=jnp.int32)
    visible = jnp.where((position < prefix_cap)[None, :], (position < length)[None, :], (position - prefix_cap)[None, :] <= row_index[:, None])
    scores = jnp.where(visible[None], scores, -1e30)
    highest = jnp.max(scores, axis=-1, keepdims=True)
    weights = jnp.exp(scores - highest)
    probs = (weights / jnp.sum(weights, axis=-1, keepdims=True)).astype(jnp.bfloat16)
    context = jnp.einsum("hnk,kc->nhc", probs.astype(jnp.float32), keys_f[:, :LATENT])
    return context.reshape(NEW, H * LATENT).astype(jnp.bfloat16)


def reference(latent_pool, page_owner, page_slot, prefix_len, queries, new_latent, tokens, expert_ids, gates, w_gate, w_up, w_down):
    page_rows = (page_owner * POOL_DEV + page_slot).astype(jnp.int32)
    cached = latent_pool[page_rows].reshape(REQUESTS, MAXP * PAGE, LAT)
    keys_all = jnp.concatenate([cached, new_latent.reshape(REQUESTS, NEW, LAT)], axis=1)
    context = lax.map(attend, (queries, keys_all, prefix_len))

    ref_expert = expert_ids.reshape(-1)
    source_row = jnp.arange(TOKENS * TOP, dtype=jnp.int32) // TOP
    onehot = (ref_expert[:, None] == jnp.arange(EXPERTS, dtype=jnp.int32)[None, :]).astype(jnp.int32)
    order_in = jnp.sum((jnp.cumsum(onehot, axis=0) - onehot) * onehot, axis=1)
    room_size = SLICES * CAP
    dest_slot = (ref_expert * room_size + order_in).astype(jnp.int32)
    slot_source = jnp.zeros((EXPERTS * room_size,), jnp.int32).at[dest_slot].set(source_row)
    gathered = tokens[slot_source].reshape(EXPERTS, room_size, D)

    def one_expert(expert_idx):
        inputs = gathered[expert_idx]
        running = jnp.zeros((room_size, D), jnp.float32)
        for slice_idx in range(SPLIT):
            row = expert_idx * SPLIT + slice_idx
            gate_val = jnp.dot(inputs, w_gate[row], preferred_element_type=jnp.float32)
            upward = jnp.dot(inputs, w_up[row], preferred_element_type=jnp.float32)
            hidden = (jax.nn.silu(gate_val) * upward).astype(jnp.bfloat16)
            part_out = jnp.dot(hidden, w_down[row], preferred_element_type=jnp.float32).astype(jnp.bfloat16)
            running = running + part_out.astype(jnp.float32)
        return running

    expert_outs = lax.map(one_expert, jnp.arange(EXPERTS, dtype=jnp.int32))
    picked = expert_outs.reshape(EXPERTS * room_size, D)[dest_slot].reshape(TOKENS, TOP, D)
    moe_out = jnp.sum(picked * gates[:, :, None], axis=1).astype(jnp.bfloat16)
    return (context, moe_out)
```

```python
import jax
import jax.numpy as jnp
from jax import lax
from jax.experimental import pallas as pl
from jax.experimental.pallas import tpu as pltpu
from jax.sharding import PartitionSpec as P

LATENT = 512
ROPE = 64
LAT = LATENT + ROPE
EXPERTS = 16
WINDOW = 640
LOG2E = 1.4426950408889634
SCALE = 192.0 ** (-0.5)
VMEM_LIMIT = 48 * 1024 * 1024


def attend_kernel(length_ref, q_ref, even_ref, odd_ref, o_ref):
    length = length_ref[pl.program_id(0)]
    new_rows = q_ref.shape[1]
    pairs = q_ref.shape[2] // (2 * LAT)
    values = even_ref[0, :, :LATENT]
    for half, (key_ref, start) in enumerate(((even_ref, 0), (odd_ref, LATENT))):
        rows = jnp.concatenate(
            [q_ref[0, :, p * 2 * LAT + start : p * 2 * LAT + start + WINDOW] for p in range(pairs)],
            axis=0,
        )
        scores = lax.dot_general(
            rows, key_ref[0], (((1,), (1,)), ((), ())), preferred_element_type=jnp.float32
        )
        prefix_cap = scores.shape[1] - new_rows
        position = lax.broadcasted_iota(jnp.int32, scores.shape, 1)
        row = lax.rem(lax.broadcasted_iota(jnp.int32, scores.shape, 0), new_rows)
        visible = jnp.logical_or(
            position < length,
            jnp.logical_and(position >= prefix_cap, position - prefix_cap <= row),
        )
        scores = jnp.where(visible, scores, -1e30)
        highest = jnp.max(scores, axis=-1, keepdims=True)
        weights = jnp.exp2((scores - highest) * (SCALE * LOG2E))
        total = jnp.sum(weights, axis=-1, keepdims=True)
        probs = (weights * (1.0 / total)).astype(jnp.bfloat16)
        context = jnp.dot(probs, values, preferred_element_type=jnp.float32).astype(o_ref.dtype)
        for p in range(pairs):
            at = (2 * p + half) * LATENT
            o_ref[0, :, at : at + LATENT] = context[p * new_rows : (p + 1) * new_rows]


def attend(queries, keys, prefix_len):
    requests, new_rows, width = queries.shape
    heads = width // LAT
    block = 16 if heads % 16 == 0 else 2
    key_rows = keys.shape[1]
    even = jnp.pad(keys, ((0, 0), (0, 0), (0, WINDOW - LAT)))
    odd = jnp.pad(keys, ((0, 0), (0, 0), (WINDOW - LAT, 0)))
    key_spec = pl.BlockSpec((1, key_rows, WINDOW), lambda r, h, *_: (r, 0, 0))
    return pl.pallas_call(
        attend_kernel,
        out_shape=jax.ShapeDtypeStruct((requests, new_rows, heads * LATENT), jnp.bfloat16),
        grid_spec=pltpu.PrefetchScalarGridSpec(
            num_scalar_prefetch=1,
            grid=(requests, heads // block),
            in_specs=[
                pl.BlockSpec((1, new_rows, block * LAT), lambda r, h, *_: (r, 0, h)),
                key_spec,
                key_spec,
            ],
            out_specs=pl.BlockSpec((1, new_rows, block * LATENT), lambda r, h, *_: (r, 0, h)),
        ),
        compiler_params=pltpu.CompilerParams(vmem_limit_bytes=VMEM_LIMIT),
        cost_estimate=pl.CostEstimate(
            flops=2 * requests * new_rows * heads * key_rows * (LAT + LATENT),
            bytes_accessed=2 * requests * new_rows * heads * (LAT + LATENT),
            transcendentals=requests * new_rows * heads * key_rows,
        ),
    )(prefix_len, queries, even, odd)


def mlp_kernel(x_ref, gate_ref, up_ref, down_ref, o_ref, total):
    step = pl.program_id(0)
    x = x_ref[...]
    gate_val = jnp.dot(x, gate_ref[0], preferred_element_type=jnp.float32)
    upward = jnp.dot(x, up_ref[0], preferred_element_type=jnp.float32)
    hidden = (gate_val / (1.0 + jnp.exp(-gate_val)) * upward).astype(jnp.bfloat16)
    columns = 512
    for c in range(0, o_ref.shape[1], columns):
        product = jnp.dot(
            hidden, down_ref[0, :, c : c + columns], preferred_element_type=jnp.float32
        )

        @pl.when(step == 0)
        def _():
            total[:, c : c + columns] = product

        @pl.when(step > 0)
        def _():
            total[:, c : c + columns] += product

    @pl.when(step == pl.num_programs(0) - 1)
    def _():
        o_ref[...] = total[...].astype(o_ref.dtype)


def expert_mlp(x, w_gate, w_up, w_down):
    rows, features = x.shape
    units = w_gate.shape[2]
    tile = min(256, units)
    whole = pl.BlockSpec((rows, features), lambda i: (0, 0), pipeline_mode=pl.Buffered(1))
    return pl.pallas_call(
        mlp_kernel,
        out_shape=jax.ShapeDtypeStruct((rows, features), jnp.bfloat16),
        grid=(units // tile,),
        in_specs=[
            whole,
            pl.BlockSpec((1, features, tile), lambda i: (0, 0, i)),
            pl.BlockSpec((1, features, tile), lambda i: (0, 0, i)),
            pl.BlockSpec((1, tile, features), lambda i: (0, i, 0)),
        ],
        out_specs=pl.BlockSpec((rows, features), lambda i: (0, 0)),
        scratch_shapes=[pltpu.VMEM((rows, features), jnp.float32)],
        compiler_params=pltpu.CompilerParams(vmem_limit_bytes=VMEM_LIMIT),
        cost_estimate=pl.CostEstimate(
            flops=6 * rows * features * units,
            bytes_accessed=6 * features * units + 4 * rows * features,
            transcendentals=rows * units,
        ),
    )(x, w_gate, w_up, w_down)


def per_device(
    latent_pool,
    page_owner,
    page_slot,
    prefix_len,
    queries,
    new_latent,
    tokens,
    expert_ids,
    gates,
    w_gate,
    w_up,
    w_down,
):
    owner_count = lax.axis_size("expert")
    dp_count = lax.axis_size("dp")
    request_count, page_count = page_owner.shape
    pool_rows, page_width = latent_pool.shape
    page_rows = page_width // LAT
    token_rows, features = tokens.shape
    top_count = expert_ids.shape[1]
    capacity = 3 * token_rows * top_count // (2 * EXPERTS)
    slice_count = owner_count * dp_count
    split_count = slice_count // EXPERTS
    both = ("expert", "dp")

    all_ids = lax.all_gather(expert_ids, both, axis=0, tiled=False)
    all_tokens = lax.all_gather(tokens, both, axis=0, tiled=True)
    pool = lax.all_gather(latent_pool, "expert", axis=0, tiled=True)

    mine = (lax.axis_index("expert") * dp_count + lax.axis_index("dp")) // split_count
    named = jnp.any(all_ids == mine, axis=2).astype(jnp.bfloat16)
    earlier = (jnp.arange(token_rows)[:, None] < jnp.arange(token_rows)[None, :]).astype(jnp.bfloat16)
    rank = jnp.dot(named, earlier, preferred_element_type=jnp.float32).astype(jnp.int32)
    place = jnp.arange(slice_count, dtype=jnp.int32)[:, None] * capacity + rank
    place = jnp.where(named > 0, place, -1).reshape(-1)
    dispatch = (
        jnp.arange(slice_count * capacity, dtype=jnp.int32)[:, None] == place[None, :]
    ).astype(jnp.bfloat16)
    received = jnp.dot(dispatch, all_tokens, preferred_element_type=jnp.float32).astype(jnp.bfloat16)
    parts = expert_mlp(received, w_gate, w_up, w_down)
    returned = lax.all_to_all(
        parts.reshape(slice_count, capacity, features), both, split_axis=0, concat_axis=0, tiled=True
    )

    page_at = (page_owner * pool_rows + page_slot).reshape(-1)
    cached = pool.at[page_at].get(mode="promise_in_bounds").reshape(
        request_count, page_count * page_rows, LAT
    )
    keys = jnp.concatenate([cached, new_latent.reshape(request_count, -1, LAT)], axis=1)
    context = attend(queries, keys, prefix_len)

    own_rows = jnp.arange(token_rows * top_count) // top_count
    chosen = (expert_ids.reshape(-1)[:, None] == jnp.arange(EXPERTS)[None, :]).astype(jnp.float32)
    tokens_before = (own_rows[None, :] < own_rows[:, None]).astype(jnp.float32)
    own_rank = jnp.sum(jnp.dot(tokens_before, chosen) * chosen, axis=1).astype(jnp.int32)
    dest = (expert_ids.reshape(-1) * capacity + own_rank).reshape(token_rows, top_count)
    weighting = jnp.sum(
        jnp.where(
            dest[:, :, None] == jnp.arange(EXPERTS * capacity, dtype=jnp.int32)[None, None, :],
            gates[:, :, None],
            0.0,
        ),
        axis=1,
    )
    returned = returned.reshape(EXPERTS, split_count, capacity, features)
    summed = jnp.sum(returned, axis=1, dtype=jnp.float32).reshape(EXPERTS * capacity, features)
    moe_out = jnp.dot(
        weighting, summed, precision=lax.Precision.HIGHEST, preferred_element_type=jnp.float32
    ).astype(jnp.bfloat16)
    return (context, moe_out)


def solution(mesh):
    return jax.shard_map(
        per_device,
        mesh=mesh,
        in_specs=(
            P(("groups", "expert"), None),
            P(("groups", "expert"), None),
            P(("groups", "expert"), None),
            P(("groups", "expert")),
            P(("groups", "expert"), None, "dp"),
            P(("groups", "expert"), None),
            P(("groups", "expert", "dp"), None),
            P(("groups", "expert", "dp"), None),
            P(("groups", "expert", "dp"), None),
            P(("expert", "dp"), None, None),
            P(("expert", "dp"), None, None),
            P(("expert", "dp"), None, None),
        ),
        out_specs=(P(("groups", "expert"), None, "dp"), P(("groups", "expert", "dp"), None)),
        check_vma=False,
    )
```

```python
import jax
import jax.numpy as jnp
from jax import lax
from jax.experimental import pallas as pl
from jax.experimental.pallas import tpu as pltpu
from jax.sharding import PartitionSpec as P

LATENT = 512
ROPE = 64
LAT = LATENT + ROPE
EXPERTS = 16
CAPP = 2
ASK_LANES = 128
WINDOW = 640
LOG2E = 1.4426950408889634
SCALE = 192.0 ** (-0.5)
VMEM_LIMIT = 48 * 1024 * 1024


def attend_kernel(length_ref, q_ref, even_ref, odd_ref, o_ref):
    length = length_ref[pl.program_id(0)]
    new_rows = q_ref.shape[1]
    pairs = q_ref.shape[2] // (2 * LAT)
    values = even_ref[0, :, :LATENT]
    for half, (key_ref, start) in enumerate(((even_ref, 0), (odd_ref, LATENT))):
        rows = jnp.concatenate(
            [q_ref[0, :, p * 2 * LAT + start : p * 2 * LAT + start + WINDOW] for p in range(pairs)],
            axis=0,
        )
        scores = lax.dot_general(
            rows, key_ref[0], (((1,), (1,)), ((), ())), preferred_element_type=jnp.float32
        )
        prefix_cap = scores.shape[1] - new_rows
        position = lax.broadcasted_iota(jnp.int32, scores.shape, 1)
        row = lax.rem(lax.broadcasted_iota(jnp.int32, scores.shape, 0), new_rows)
        visible = jnp.logical_or(
            position < length,
            jnp.logical_and(position >= prefix_cap, position - prefix_cap <= row),
        )
        scores = jnp.where(visible, scores, -1e30)
        highest = jnp.max(scores, axis=-1, keepdims=True)
        weights = jnp.exp2((scores - highest) * (SCALE * LOG2E))
        total = jnp.sum(weights, axis=-1, keepdims=True)
        probs = (weights * (1.0 / total)).astype(jnp.bfloat16)
        context = jnp.dot(probs, values, preferred_element_type=jnp.float32).astype(o_ref.dtype)
        for p in range(pairs):
            at = (2 * p + half) * LATENT
            o_ref[0, :, at : at + LATENT] = context[p * new_rows : (p + 1) * new_rows]


def attend(queries, keys, prefix_len):
    requests, new_rows, width = queries.shape
    heads = width // LAT
    block = 16 if heads % 16 == 0 else 2
    key_rows = keys.shape[1]
    even = jnp.pad(keys, ((0, 0), (0, 0), (0, WINDOW - LAT)))
    odd = jnp.pad(keys, ((0, 0), (0, 0), (WINDOW - LAT, 0)))
    key_spec = pl.BlockSpec((1, key_rows, WINDOW), lambda r, h, *_: (r, 0, 0))
    return pl.pallas_call(
        attend_kernel,
        out_shape=jax.ShapeDtypeStruct((requests, new_rows, heads * LATENT), jnp.bfloat16),
        grid_spec=pltpu.PrefetchScalarGridSpec(
            num_scalar_prefetch=1,
            grid=(requests, heads // block),
            in_specs=[
                pl.BlockSpec((1, new_rows, block * LAT), lambda r, h, *_: (r, 0, h)),
                key_spec,
                key_spec,
            ],
            out_specs=pl.BlockSpec((1, new_rows, block * LATENT), lambda r, h, *_: (r, 0, h)),
        ),
        compiler_params=pltpu.CompilerParams(vmem_limit_bytes=VMEM_LIMIT),
        cost_estimate=pl.CostEstimate(
            flops=2 * requests * new_rows * heads * key_rows * (LAT + LATENT),
            bytes_accessed=2 * requests * new_rows * heads * (LAT + LATENT),
            transcendentals=requests * new_rows * heads * key_rows,
        ),
    )(prefix_len, queries, even, odd)


def mlp_kernel(x_ref, gate_ref, up_ref, down_ref, o_ref, total):
    step = pl.program_id(0)
    x = x_ref[...]
    gate_val = jnp.dot(x, gate_ref[0], preferred_element_type=jnp.float32)
    upward = jnp.dot(x, up_ref[0], preferred_element_type=jnp.float32)
    hidden = (gate_val / (1.0 + jnp.exp(-gate_val)) * upward).astype(jnp.bfloat16)
    columns = 512
    for c in range(0, o_ref.shape[1], columns):
        product = jnp.dot(
            hidden, down_ref[0, :, c : c + columns], preferred_element_type=jnp.float32
        )

        @pl.when(step == 0)
        def _():
            total[:, c : c + columns] = product

        @pl.when(step > 0)
        def _():
            total[:, c : c + columns] += product

    @pl.when(step == pl.num_programs(0) - 1)
    def _():
        o_ref[...] = total[...].astype(o_ref.dtype)


def expert_mlp(x, w_gate, w_up, w_down):
    rows, features = x.shape[0], w_gate.shape[1]
    units = w_gate.shape[2]
    tile = min(256, units)
    whole = pl.BlockSpec((rows, features), lambda i: (0, 0), pipeline_mode=pl.Buffered(1))
    return pl.pallas_call(
        mlp_kernel,
        out_shape=jax.ShapeDtypeStruct((rows, features), jnp.bfloat16),
        grid=(units // tile,),
        in_specs=[
            whole,
            pl.BlockSpec((1, features, tile), lambda i: (0, 0, i)),
            pl.BlockSpec((1, features, tile), lambda i: (0, 0, i)),
            pl.BlockSpec((1, tile, features), lambda i: (0, i, 0)),
        ],
        out_specs=pl.BlockSpec((rows, features), lambda i: (0, 0)),
        scratch_shapes=[pltpu.VMEM((rows, features), jnp.float32)],
        compiler_params=pltpu.CompilerParams(vmem_limit_bytes=VMEM_LIMIT),
        cost_estimate=pl.CostEstimate(
            flops=6 * rows * features * units,
            bytes_accessed=6 * features * units + 4 * rows * features,
            transcendentals=rows * units,
        ),
    )(x, w_gate, w_up, w_down)


def per_device(
    latent_pool,
    page_owner,
    page_slot,
    prefix_len,
    queries,
    new_latent,
    tokens,
    expert_ids,
    gates,
    w_gate,
    w_up,
    w_down,
):
    owner_count = lax.axis_size("expert")
    dp_count = lax.axis_size("dp")
    request_count, page_count = page_owner.shape
    pool_rows, page_width = latent_pool.shape
    page_rows = page_width // LAT
    token_rows, features = tokens.shape
    top_count = expert_ids.shape[1]
    capacity = 3 * token_rows * top_count // (2 * EXPERTS)
    slice_count = owner_count * dp_count
    split_count = slice_count // EXPERTS
    both = ("expert", "dp")

    wanted = jnp.any(
        expert_ids[:, :, None] == jnp.arange(EXPERTS, dtype=jnp.int32)[None, None, :], axis=1
    ).astype(jnp.bfloat16)
    before = (
        jnp.arange(token_rows)[:, None] > jnp.arange(token_rows)[None, :]
    ).astype(jnp.bfloat16)
    rank = jnp.dot(before, wanted, preferred_element_type=jnp.float32).astype(jnp.int32)
    place = jnp.where(
        wanted > 0, rank + capacity * jnp.arange(EXPERTS, dtype=jnp.int32)[None, :], -1
    )
    chosen = place.T[:, None, :] == jnp.arange(EXPERTS * capacity, dtype=jnp.int32).reshape(
        EXPERTS, capacity, 1
    )
    dispatch = chosen.reshape(EXPERTS * capacity, token_rows).astype(jnp.bfloat16)
    buffer = jnp.dot(dispatch, tokens, preferred_element_type=jnp.float32).astype(jnp.bfloat16)

    refs_owner = page_owner.reshape(-1)
    named = refs_owner[:, None] == jnp.arange(owner_count, dtype=jnp.int32)[None, :]
    ref_at = jnp.arange(refs_owner.shape[0], dtype=jnp.int32)
    same = (refs_owner[:, None] == refs_owner[None, :]) & (ref_at[None, :] < ref_at[:, None])
    ref_rank = jnp.sum(same.astype(jnp.int32), axis=1)
    asks = jnp.sum(
        jnp.where(
            named[:, :, None]
            & (ref_rank[:, None, None] == jnp.arange(ASK_LANES, dtype=jnp.int32)[None, None, :]),
            page_slot.reshape(-1)[:, None, None],
            0,
        ),
        axis=0,
    ).astype(jnp.bfloat16)
    asks = jnp.repeat(asks, dp_count, axis=0)
    outgoing = jnp.broadcast_to(
        buffer.reshape(EXPERTS, 1, capacity, features), (EXPERTS, split_count, capacity, features)
    ).reshape(slice_count, capacity, features)
    outgoing = jnp.concatenate(
        [outgoing, jnp.broadcast_to(asks[:, None, :], (slice_count, capacity, ASK_LANES))], axis=2
    )
    received = lax.all_to_all(outgoing, both, split_axis=0, concat_axis=0, tiled=True)

    asked = received[:, 0, features : features + CAPP].reshape(owner_count, dp_count, CAPP)[:, 0]
    lines = latent_pool.reshape(pool_rows, page_width // 128, 128)
    fetched = lines.at[asked.astype(jnp.int32)].get(mode="clip")
    arrived = lax.all_to_all(fetched, "expert", split_axis=0, concat_axis=0, tiled=True)

    parts = expert_mlp(received.reshape(-1, features + ASK_LANES), w_gate, w_up, w_down)
    parts, arrived = lax.optimization_barrier((parts, arrived))
    returned = lax.all_to_all(
        parts.reshape(slice_count, capacity, features), both, split_axis=0, concat_axis=0, tiled=True
    )

    page_at = refs_owner * CAPP + ref_rank
    cached = (
        arrived.reshape(owner_count * CAPP, page_width // 128, 128)
        .at[page_at]
        .get(mode="clip")
        .reshape(request_count, page_count * page_rows, LAT)
    )
    keys = jnp.concatenate([cached, new_latent.reshape(request_count, -1, LAT)], axis=1)
    context = attend(queries, keys, prefix_len)

    summed = returned.reshape(EXPERTS, split_count, capacity, features)
    summed = jnp.sum(summed, axis=1, dtype=jnp.float32).reshape(EXPERTS * capacity, features)
    weight = jnp.sum(
        jnp.where(
            expert_ids[:, :, None] == jnp.arange(EXPERTS, dtype=jnp.int32)[None, None, :],
            gates[:, :, None],
            0.0,
        ),
        axis=1,
    )
    weighting = jnp.where(chosen, weight.T[:, None, :], 0.0).reshape(
        EXPERTS * capacity, token_rows
    )
    moe_out = lax.dot_general(
        weighting,
        summed,
        (((0,), (0,)), ((), ())),
        precision=lax.Precision.HIGHEST,
        preferred_element_type=jnp.float32,
    ).astype(jnp.bfloat16)
    return (context, moe_out)


def solution(mesh):
    return jax.shard_map(
        per_device,
        mesh=mesh,
        in_specs=(
            P(("groups", "expert"), None),
            P(("groups", "expert"), None),
            P(("groups", "expert"), None),
            P(("groups", "expert")),
            P(("groups", "expert"), None, "dp"),
            P(("groups", "expert"), None),
            P(("groups", "expert", "dp"), None),
            P(("groups", "expert", "dp"), None),
            P(("groups", "expert", "dp"), None),
            P(("expert", "dp"), None, None),
            P(("expert", "dp"), None, None),
            P(("expert", "dp"), None, None),
        ),
        out_specs=(P(("groups", "expert"), None, "dp"), P(("groups", "expert", "dp"), None)),
        check_vma=False,
    )
```

```python
import functools

import jax
import jax.numpy as jnp
from jax import lax
from jax.experimental import pallas as pl
from jax.experimental.pallas import tpu as pltpu
from jax.sharding import PartitionSpec as P

LATENT = 512
ROPE = 64
LAT = LATENT + ROPE
EXPERTS = 16
CAPP = 2
ASK_LANES = 128
WINDOW = 640
LOG2E = 1.4426950408889634
SCALE = 192.0 ** (-0.5)
VMEM_LIMIT = 48 * 1024 * 1024


def attend_kernel(length_ref, q_ref, even_ref, odd_ref, o_ref):
    length = length_ref[pl.program_id(0)]
    new_rows = q_ref.shape[1]
    pairs = q_ref.shape[2] // (2 * LAT)
    values = even_ref[0, :, :LATENT]
    for half, (key_ref, start) in enumerate(((even_ref, 0), (odd_ref, LATENT))):
        rows = jnp.concatenate(
            [q_ref[0, :, p * 2 * LAT + start : p * 2 * LAT + start + WINDOW] for p in range(pairs)],
            axis=0,
        )
        scores = lax.dot_general(
            rows, key_ref[0], (((1,), (1,)), ((), ())), preferred_element_type=jnp.float32
        )
        prefix_cap = scores.shape[1] - new_rows
        position = lax.broadcasted_iota(jnp.int32, scores.shape, 1)
        row = lax.rem(lax.broadcasted_iota(jnp.int32, scores.shape, 0), new_rows)
        visible = jnp.logical_or(
            position < length,
            jnp.logical_and(position >= prefix_cap, position - prefix_cap <= row),
        )
        scores = jnp.where(visible, scores, -1e30)
        highest = jnp.max(scores, axis=-1, keepdims=True)
        weights = jnp.exp2((scores - highest) * (SCALE * LOG2E))
        total = jnp.sum(weights, axis=-1, keepdims=True)
        probs = (weights * (1.0 / total)).astype(jnp.bfloat16)
        context = jnp.dot(probs, values, preferred_element_type=jnp.float32).astype(o_ref.dtype)
        for p in range(pairs):
            at = (2 * p + half) * LATENT
            o_ref[0, :, at : at + LATENT] = context[p * new_rows : (p + 1) * new_rows]


def attend(queries, keys, prefix_len):
    requests, new_rows, width = queries.shape
    heads = width // LAT
    block = 16 if heads % 16 == 0 else 2
    key_rows = keys.shape[1]
    even = jnp.pad(keys, ((0, 0), (0, 0), (0, WINDOW - LAT)))
    odd = jnp.pad(keys, ((0, 0), (0, 0), (WINDOW - LAT, 0)))
    key_spec = pl.BlockSpec((1, key_rows, WINDOW), lambda r, h, *_: (r, 0, 0))
    return pl.pallas_call(
        attend_kernel,
        out_shape=jax.ShapeDtypeStruct((requests, new_rows, heads * LATENT), jnp.bfloat16),
        grid_spec=pltpu.PrefetchScalarGridSpec(
            num_scalar_prefetch=1,
            grid=(requests, heads // block),
            in_specs=[
                pl.BlockSpec((1, new_rows, block * LAT), lambda r, h, *_: (r, 0, h)),
                key_spec,
                key_spec,
            ],
            out_specs=pl.BlockSpec((1, new_rows, block * LATENT), lambda r, h, *_: (r, 0, h)),
        ),
        compiler_params=pltpu.CompilerParams(vmem_limit_bytes=VMEM_LIMIT),
        cost_estimate=pl.CostEstimate(
            flops=2 * requests * new_rows * heads * key_rows * (LAT + LATENT),
            bytes_accessed=2 * requests * new_rows * heads * (LAT + LATENT),
            transcendentals=requests * new_rows * heads * key_rows,
        ),
    )(prefix_len, queries, even, odd)


def mlp_kernel(x_ref, gate_ref, up_ref, down_ref, o_ref, total):
    step = pl.program_id(0)
    x = x_ref[...]
    gate_val = jnp.dot(x, gate_ref[0], preferred_element_type=jnp.float32)
    upward = jnp.dot(x, up_ref[0], preferred_element_type=jnp.float32)
    hidden = (gate_val / (1.0 + jnp.exp(-gate_val)) * upward).astype(jnp.bfloat16)
    columns = 512
    for c in range(0, o_ref.shape[1], columns):
        product = jnp.dot(
            hidden, down_ref[0, :, c : c + columns], preferred_element_type=jnp.float32
        )

        @pl.when(step == 0)
        def _():
            total[:, c : c + columns] = product

        @pl.when(step > 0)
        def _():
            total[:, c : c + columns] += product

    @pl.when(step == pl.num_programs(0) - 1)
    def _():
        o_ref[...] = total[...].astype(o_ref.dtype)


def expert_mlp(x, w_gate, w_up, w_down):
    rows, features = x.shape[0], w_gate.shape[1]
    units = w_gate.shape[2]
    tile = min(256, units)
    whole = pl.BlockSpec((rows, features), lambda i: (0, 0), pipeline_mode=pl.Buffered(1))
    return pl.pallas_call(
        mlp_kernel,
        out_shape=jax.ShapeDtypeStruct((rows, features), jnp.bfloat16),
        grid=(units // tile,),
        in_specs=[
            whole,
            pl.BlockSpec((1, features, tile), lambda i: (0, 0, i)),
            pl.BlockSpec((1, features, tile), lambda i: (0, 0, i)),
            pl.BlockSpec((1, tile, features), lambda i: (0, i, 0)),
        ],
        out_specs=pl.BlockSpec((rows, features), lambda i: (0, 0)),
        scratch_shapes=[pltpu.VMEM((rows, features), jnp.float32)],
        compiler_params=pltpu.CompilerParams(vmem_limit_bytes=VMEM_LIMIT),
        cost_estimate=pl.CostEstimate(
            flops=6 * rows * features * units,
            bytes_accessed=6 * features * units + 4 * rows * features,
            transcendentals=rows * units,
        ),
    )(x, w_gate, w_up, w_down)


def gather_kernel(n, dp_count, own_ref, all_ref, local_sem, ring_out, ring_in, pair_out, pair_in):
    flat = lax.axis_index("expert") * dp_count + lax.axis_index("dp")
    group = lax.axis_index("groups")
    chip, core = lax.div(flat, 2), lax.rem(flat, 2)
    if dp_count == 1:
        column, level = lax.rem(chip, 2), lax.div(chip, 2)
        place = level + column * (n - 1 - 2 * level)
    else:
        place = chip

    def at(offset):
        q = lax.rem(place + offset + n, n)
        if dp_count == 1:
            down = lax.div(q, n // 2)
            q = 2 * (q + down * (n - 1 - 2 * q)) + down
        return 2 * q + core

    def copy(src, block, send, recv, target):
        return pltpu.make_async_remote_copy(
            src_ref=src,
            dst_ref=all_ref.at[block],
            send_sem=send,
            recv_sem=recv,
            device_id=(group, lax.div(target, dp_count), lax.rem(target, dp_count)),
            device_id_type=pl.DeviceIdType.MESH,
        )

    right, left, other = at(1), at(-1), flat + 1 - 2 * core
    barrier = pltpu.get_barrier_semaphore()
    for target in (right, left, other):
        pl.semaphore_signal(
            barrier,
            inc=1,
            device_id=(group, lax.div(target, dp_count), lax.rem(target, dp_count)),
            device_id_type=pl.DeviceIdType.MESH,
        )
    pl.semaphore_wait(barrier, 3)

    hops = (n // 2, n - 1 - n // 2)
    ring, pair = {}, []

    def ring_start(way, hop, src, block):
        k = hop + way * hops[0]
        ring[way, hop] = copy(src, block, ring_out.at[k], ring_in.at[k], (right, left)[way])
        ring[way, hop].start()

    def pair_start(src, block):
        j = len(pair)
        pair.append(copy(src, block, pair_out.at[j], pair_in.at[j], other))
        pair[-1].start()

    ring_start(0, 0, own_ref, flat)
    ring_start(1, 0, own_ref, flat)
    local = pltpu.make_async_copy(own_ref, all_ref.at[flat], local_sem)
    local.start()
    pair_start(own_ref, flat)
    for hop in range(hops[0]):
        for way in (0, 1):
            if hop < hops[way]:
                block = at((-1, 1)[way] * (hop + 1))
                ring[way, hop].wait_recv()
                if hop + 1 < hops[way]:
                    ring_start(way, hop + 1, all_ref.at[block], block)
                pair_start(all_ref.at[block], block)
    for sent in ring.values():
        sent.wait_send()
    for sent in pair:
        sent.wait()
    local.wait()


def gather_all(block, dp_count, count):
    n = count // 2
    return pl.pallas_call(
        functools.partial(gather_kernel, n, dp_count),
        out_shape=jax.ShapeDtypeStruct((count,) + block.shape, block.dtype),
        in_specs=[pl.BlockSpec(memory_space=pl.ANY)],
        out_specs=pl.BlockSpec(memory_space=pl.ANY),
        scratch_shapes=[
            pltpu.SemaphoreType.DMA,
            pltpu.SemaphoreType.DMA((n - 1,)),
            pltpu.SemaphoreType.DMA((n - 1,)),
            pltpu.SemaphoreType.DMA((n,)),
            pltpu.SemaphoreType.DMA((n,)),
        ],
        compiler_params=pltpu.CompilerParams(collective_id=0, has_side_effects=True),
    )(block)


def per_device(
    latent_pool,
    page_owner,
    page_slot,
    prefix_len,
    queries,
    new_latent,
    tokens,
    expert_ids,
    gates,
    w_gate,
    w_up,
    w_down,
):
    owner_count = lax.axis_size("expert")
    dp_count = lax.axis_size("dp")
    request_count, page_count = page_owner.shape
    pool_rows, page_width = latent_pool.shape
    page_rows = page_width // LAT
    token_rows, features = tokens.shape
    top_count = expert_ids.shape[1]
    capacity = 3 * token_rows * top_count // (2 * EXPERTS)
    slice_count = owner_count * dp_count
    split_count = slice_count // EXPERTS
    both = ("expert", "dp")

    wanted = jnp.any(
        expert_ids[:, :, None] == jnp.arange(EXPERTS, dtype=jnp.int32)[None, None, :], axis=1
    ).astype(jnp.bfloat16)
    before = (
        jnp.arange(token_rows)[:, None] > jnp.arange(token_rows)[None, :]
    ).astype(jnp.bfloat16)
    rank = jnp.dot(before, wanted, preferred_element_type=jnp.float32).astype(jnp.int32)
    place = jnp.where(
        wanted > 0, rank + capacity * jnp.arange(EXPERTS, dtype=jnp.int32)[None, :], -1
    )
    chosen = place.T[:, None, :] == jnp.arange(EXPERTS * capacity, dtype=jnp.int32).reshape(
        EXPERTS, capacity, 1
    )

    refs_owner = page_owner.reshape(-1)
    named = refs_owner[:, None] == jnp.arange(owner_count, dtype=jnp.int32)[None, :]
    ref_at = jnp.arange(refs_owner.shape[0], dtype=jnp.int32)
    same = (refs_owner[:, None] == refs_owner[None, :]) & (ref_at[None, :] < ref_at[:, None])
    ref_rank = jnp.sum(same.astype(jnp.int32), axis=1)
    asks = jnp.sum(
        jnp.where(
            named[:, :, None]
            & (ref_rank[:, None, None] == jnp.arange(CAPP, dtype=jnp.int32)[None, None, :]),
            page_slot.reshape(-1)[:, None, None],
            0,
        ),
        axis=0,
    ).astype(jnp.bfloat16)
    extra = jnp.concatenate(
        [
            expert_ids.astype(jnp.bfloat16),
            jnp.broadcast_to(asks.reshape(1, -1), (token_rows, owner_count * CAPP)),
        ],
        axis=1,
    )
    extra = jnp.pad(extra, ((0, 0), (0, ASK_LANES - extra.shape[1])))
    gathered = gather_all(jnp.concatenate([tokens, extra], axis=1), dp_count, slice_count)

    me = lax.axis_index("expert")
    first = gathered[:, 0, features:].reshape(owner_count, dp_count, ASK_LANES)[:, 0]
    asked = first[:, top_count : top_count + owner_count * CAPP]
    asked = lax.dynamic_index_in_dim(
        asked.reshape(owner_count, owner_count, CAPP), me, axis=1, keepdims=False
    )

    mine = ((me * dp_count + lax.axis_index("dp")) // split_count).astype(jnp.bfloat16)
    routed = jnp.any(gathered[:, :, features : features + top_count] == mine, axis=2)
    rank_in = jnp.dot(
        routed.astype(jnp.bfloat16), before.T, preferred_element_type=jnp.float32
    ).astype(jnp.int32)
    place_in = jnp.arange(slice_count, dtype=jnp.int32)[:, None] * capacity + rank_in
    place_in = jnp.where(routed, place_in, -1).reshape(-1)
    dispatch = (
        jnp.arange(slice_count * capacity, dtype=jnp.int32)[:, None] == place_in[None, :]
    ).astype(jnp.bfloat16)
    lines = latent_pool.reshape(pool_rows, page_width // 128, 128)
    fetched = lines.at[asked.astype(jnp.int32)].get(mode="clip")
    arrived = lax.all_to_all(fetched, "expert", split_axis=0, concat_axis=0, tiled=True)

    received = jnp.dot(
        dispatch, gathered.reshape(slice_count * token_rows, -1), preferred_element_type=jnp.float32
    ).astype(jnp.bfloat16)
    parts = expert_mlp(received, w_gate, w_up, w_down)
    parts, arrived = lax.optimization_barrier((parts, arrived))
    returned = lax.all_to_all(
        parts.reshape(slice_count, capacity, features), both, split_axis=0, concat_axis=0, tiled=True
    )

    page_at = refs_owner * CAPP + ref_rank
    cached = (
        arrived.reshape(owner_count * CAPP, page_width // 128, 128)
        .at[page_at]
        .get(mode="clip")
        .reshape(request_count, page_count * page_rows, LAT)
    )
    keys = jnp.concatenate([cached, new_latent.reshape(request_count, -1, LAT)], axis=1)
    context = attend(queries, keys, prefix_len)

    summed = returned.reshape(EXPERTS, split_count, capacity, features)
    summed = jnp.sum(summed, axis=1, dtype=jnp.float32).reshape(EXPERTS * capacity, features)
    weight = jnp.sum(
        jnp.where(
            expert_ids[:, :, None] == jnp.arange(EXPERTS, dtype=jnp.int32)[None, None, :],
            gates[:, :, None],
            0.0,
        ),
        axis=1,
    )
    weighting = jnp.where(chosen, weight.T[:, None, :], 0.0).reshape(
        EXPERTS * capacity, token_rows
    )
    moe_out = lax.dot_general(
        weighting,
        summed,
        (((0,), (0,)), ((), ())),
        precision=lax.Precision.HIGHEST,
        preferred_element_type=jnp.float32,
    ).astype(jnp.bfloat16)
    return (context, moe_out)


def solution(mesh):
    return jax.shard_map(
        per_device,
        mesh=mesh,
        in_specs=(
            P(("groups", "expert"), None),
            P(("groups", "expert"), None),
            P(("groups", "expert"), None),
            P(("groups", "expert")),
            P(("groups", "expert"), None, "dp"),
            P(("groups", "expert"), None),
            P(("groups", "expert", "dp"), None),
            P(("groups", "expert", "dp"), None),
            P(("groups", "expert", "dp"), None),
            P(("expert", "dp"), None, None),
            P(("expert", "dp"), None, None),
            P(("expert", "dp"), None, None),
        ),
        out_specs=(P(("groups", "expert"), None, "dp"), P(("groups", "expert", "dp"), None)),
        check_vma=False,
    )
```

```python
import functools

import jax
import jax.numpy as jnp
from jax import lax
from jax.experimental import pallas as pl
from jax.experimental.pallas import tpu as pltpu
from jax.sharding import PartitionSpec as P

LATENT = 512
ROPE = 64
LAT = LATENT + ROPE
EXPERTS = 16
CAPP = 2
ASK_LANES = 128
CHUNKS = 2
WINDOW = 640
LOG2E = 1.4426950408889634
SCALE = 192.0 ** (-0.5)
VMEM_LIMIT = 48 * 1024 * 1024


def attend_kernel(length_ref, q_ref, even_ref, odd_ref, o_ref):
    length = length_ref[pl.program_id(0)]
    new_rows = q_ref.shape[1]
    pairs = q_ref.shape[2] // (2 * LAT)
    values = even_ref[0, :, :LATENT]
    for half, (key_ref, start) in enumerate(((even_ref, 0), (odd_ref, LATENT))):
        rows = jnp.concatenate(
            [q_ref[0, :, p * 2 * LAT + start : p * 2 * LAT + start + WINDOW] for p in range(pairs)],
            axis=0,
        )
        scores = lax.dot_general(
            rows, key_ref[0], (((1,), (1,)), ((), ())), preferred_element_type=jnp.float32
        )
        prefix_cap = scores.shape[1] - new_rows
        position = lax.broadcasted_iota(jnp.int32, scores.shape, 1)
        row = lax.rem(lax.broadcasted_iota(jnp.int32, scores.shape, 0), new_rows)
        visible = jnp.logical_or(
            position < length,
            jnp.logical_and(position >= prefix_cap, position - prefix_cap <= row),
        )
        scores = jnp.where(visible, scores, -1e30)
        highest = jnp.max(scores, axis=-1, keepdims=True)
        weights = jnp.exp2((scores - highest) * (SCALE * LOG2E))
        total = jnp.sum(weights, axis=-1, keepdims=True)
        probs = (weights * (1.0 / total)).astype(jnp.bfloat16)
        context = jnp.dot(probs, values, preferred_element_type=jnp.float32).astype(o_ref.dtype)
        for p in range(pairs):
            at = (2 * p + half) * LATENT
            o_ref[0, :, at : at + LATENT] = context[p * new_rows : (p + 1) * new_rows]


def attend(queries, keys, prefix_len):
    requests, new_rows, width = queries.shape
    heads = width // LAT
    block = 16 if heads % 16 == 0 else 2
    key_rows = keys.shape[1]
    even = jnp.pad(keys, ((0, 0), (0, 0), (0, WINDOW - LAT)))
    odd = jnp.pad(keys, ((0, 0), (0, 0), (WINDOW - LAT, 0)))
    key_spec = pl.BlockSpec((1, key_rows, WINDOW), lambda r, h, *_: (r, 0, 0))
    return pl.pallas_call(
        attend_kernel,
        out_shape=jax.ShapeDtypeStruct((requests, new_rows, heads * LATENT), jnp.bfloat16),
        grid_spec=pltpu.PrefetchScalarGridSpec(
            num_scalar_prefetch=1,
            grid=(requests, heads // block),
            in_specs=[
                pl.BlockSpec((1, new_rows, block * LAT), lambda r, h, *_: (r, 0, h)),
                key_spec,
                key_spec,
            ],
            out_specs=pl.BlockSpec((1, new_rows, block * LATENT), lambda r, h, *_: (r, 0, h)),
        ),
        compiler_params=pltpu.CompilerParams(vmem_limit_bytes=VMEM_LIMIT),
        cost_estimate=pl.CostEstimate(
            flops=2 * requests * new_rows * heads * key_rows * (LAT + LATENT),
            bytes_accessed=2 * requests * new_rows * heads * (LAT + LATENT),
            transcendentals=requests * new_rows * heads * key_rows,
        ),
    )(prefix_len, queries, even, odd)


def mlp_kernel(x_ref, gate_ref, up_ref, down_ref, o_ref, total):
    step = pl.program_id(0)
    x = x_ref[...]
    gate_val = jnp.dot(x, gate_ref[0], preferred_element_type=jnp.float32)
    upward = jnp.dot(x, up_ref[0], preferred_element_type=jnp.float32)
    hidden = (gate_val / (1.0 + jnp.exp(-gate_val)) * upward).astype(jnp.bfloat16)
    columns = 512
    for c in range(0, o_ref.shape[1], columns):
        product = jnp.dot(
            hidden, down_ref[0, :, c : c + columns], preferred_element_type=jnp.float32
        )

        @pl.when(step == 0)
        def _():
            total[:, c : c + columns] = product

        @pl.when(step > 0)
        def _():
            total[:, c : c + columns] += product

    @pl.when(step == pl.num_programs(0) - 1)
    def _():
        o_ref[...] = total[...].astype(o_ref.dtype)


def expert_mlp(x, w_gate, w_up, w_down):
    rows, features = x.shape[0], w_gate.shape[1]
    units = w_gate.shape[2]
    tile = min(256, units)
    whole = pl.BlockSpec((rows, features), lambda i: (0, 0), pipeline_mode=pl.Buffered(1))
    return pl.pallas_call(
        mlp_kernel,
        out_shape=jax.ShapeDtypeStruct((rows, features), jnp.bfloat16),
        grid=(units // tile,),
        in_specs=[
            whole,
            pl.BlockSpec((1, features, tile), lambda i: (0, 0, i)),
            pl.BlockSpec((1, features, tile), lambda i: (0, 0, i)),
            pl.BlockSpec((1, tile, features), lambda i: (0, i, 0)),
        ],
        out_specs=pl.BlockSpec((rows, features), lambda i: (0, 0)),
        scratch_shapes=[pltpu.VMEM((rows, features), jnp.float32)],
        compiler_params=pltpu.CompilerParams(vmem_limit_bytes=VMEM_LIMIT),
        cost_estimate=pl.CostEstimate(
            flops=6 * rows * features * units,
            bytes_accessed=6 * features * units + 4 * rows * features,
            transcendentals=rows * units,
        ),
    )(x, w_gate, w_up, w_down)


def gather_kernel(n, dp_count, own_ref, all_ref, local_sem, ring_out, ring_in, pair_out, pair_in):
    flat = lax.axis_index("expert") * dp_count + lax.axis_index("dp")
    group = lax.axis_index("groups")
    chip, core = lax.div(flat, 2), lax.rem(flat, 2)
    if dp_count == 1:
        column, level = lax.rem(chip, 2), lax.div(chip, 2)
        place = level + column * (n - 1 - 2 * level)
    else:
        place = chip

    def at(offset):
        q = lax.rem(place + offset + n, n)
        if dp_count == 1:
            down = lax.div(q, n // 2)
            q = 2 * (q + down * (n - 1 - 2 * q)) + down
        return 2 * q + core

    rows = own_ref.shape[0] // CHUNKS

    def piece(ref, chunk):
        return ref.at[pl.ds(chunk * rows, rows)]

    def copy(src, block, chunk, send, recv, target):
        return pltpu.make_async_remote_copy(
            src_ref=piece(src, chunk),
            dst_ref=piece(all_ref.at[block], chunk),
            send_sem=send,
            recv_sem=recv,
            device_id=(group, lax.div(target, dp_count), lax.rem(target, dp_count)),
            device_id_type=pl.DeviceIdType.MESH,
        )

    right, left, other = at(1), at(-1), flat + 1 - 2 * core
    barrier = pltpu.get_barrier_semaphore()
    for target in (right, left, other):
        pl.semaphore_signal(
            barrier,
            inc=1,
            device_id=(group, lax.div(target, dp_count), lax.rem(target, dp_count)),
            device_id_type=pl.DeviceIdType.MESH,
        )
    pl.semaphore_wait(barrier, 3)

    hops = [
        [n // 2 if way == chunk % 2 else n - 1 - n // 2 for way in (0, 1)]
        for chunk in range(CHUNKS)
    ]
    ring, pair = {}, []

    def ring_start(chunk, way, hop, src, block):
        k = len(ring)
        ring[chunk, way, hop] = copy(
            src, block, chunk, ring_out.at[k], ring_in.at[k], (right, left)[way]
        )
        ring[chunk, way, hop].start()

    def pair_start(chunk, src, block):
        j = len(pair)
        pair.append(copy(src, block, chunk, pair_out.at[j], pair_in.at[j], other))
        pair[-1].start()

    for chunk in range(CHUNKS):
        for way in (0, 1):
            ring_start(chunk, way, 0, own_ref, flat)
    local = pltpu.make_async_copy(own_ref, all_ref.at[flat], local_sem)
    local.start()
    for chunk in range(CHUNKS):
        pair_start(chunk, own_ref, flat)
    for hop in range(n // 2):
        for chunk in range(CHUNKS):
            for way in (0, 1):
                if hop < hops[chunk][way]:
                    block = at((-1, 1)[way] * (hop + 1))
                    ring[chunk, way, hop].wait_recv()
                    if hop + 1 < hops[chunk][way]:
                        ring_start(chunk, way, hop + 1, all_ref.at[block], block)
                    pair_start(chunk, all_ref.at[block], block)
    for sent in ring.values():
        sent.wait_send()
    for sent in pair:
        sent.wait()
    local.wait()


def gather_all(block, dp_count, count):
    n = count // 2
    return pl.pallas_call(
        functools.partial(gather_kernel, n, dp_count),
        out_shape=jax.ShapeDtypeStruct((count,) + block.shape, block.dtype),
        in_specs=[pl.BlockSpec(memory_space=pl.ANY)],
        out_specs=pl.BlockSpec(memory_space=pl.ANY),
        scratch_shapes=[
            pltpu.SemaphoreType.DMA,
            pltpu.SemaphoreType.DMA((CHUNKS * (n - 1),)),
            pltpu.SemaphoreType.DMA((CHUNKS * (n - 1),)),
            pltpu.SemaphoreType.DMA((CHUNKS * n,)),
            pltpu.SemaphoreType.DMA((CHUNKS * n,)),
        ],
        compiler_params=pltpu.CompilerParams(collective_id=0, has_side_effects=True),
    )(block)


def per_device(
    latent_pool,
    page_owner,
    page_slot,
    prefix_len,
    queries,
    new_latent,
    tokens,
    expert_ids,
    gates,
    w_gate,
    w_up,
    w_down,
):
    owner_count = lax.axis_size("expert")
    dp_count = lax.axis_size("dp")
    request_count, page_count = page_owner.shape
    pool_rows, page_width = latent_pool.shape
    page_rows = page_width // LAT
    token_rows, features = tokens.shape
    top_count = expert_ids.shape[1]
    capacity = 3 * token_rows * top_count // (2 * EXPERTS)
    slice_count = owner_count * dp_count
    split_count = slice_count // EXPERTS
    both = ("expert", "dp")

    wanted = jnp.any(
        expert_ids[:, :, None] == jnp.arange(EXPERTS, dtype=jnp.int32)[None, None, :], axis=1
    ).astype(jnp.bfloat16)
    before = (
        jnp.arange(token_rows)[:, None] > jnp.arange(token_rows)[None, :]
    ).astype(jnp.bfloat16)
    rank = jnp.dot(before, wanted, preferred_element_type=jnp.float32).astype(jnp.int32)
    place = jnp.where(
        wanted > 0, rank + capacity * jnp.arange(EXPERTS, dtype=jnp.int32)[None, :], -1
    )
    chosen = place.T[:, None, :] == jnp.arange(EXPERTS * capacity, dtype=jnp.int32).reshape(
        EXPERTS, capacity, 1
    )

    refs_owner = page_owner.reshape(-1)
    named = refs_owner[:, None] == jnp.arange(owner_count, dtype=jnp.int32)[None, :]
    ref_at = jnp.arange(refs_owner.shape[0], dtype=jnp.int32)
    same = (refs_owner[:, None] == refs_owner[None, :]) & (ref_at[None, :] < ref_at[:, None])
    ref_rank = jnp.sum(same.astype(jnp.int32), axis=1)
    asks = jnp.sum(
        jnp.where(
            named[:, :, None]
            & (ref_rank[:, None, None] == jnp.arange(CAPP, dtype=jnp.int32)[None, None, :]),
            page_slot.reshape(-1)[:, None, None],
            0,
        ),
        axis=0,
    ).astype(jnp.bfloat16)
    extra = jnp.concatenate(
        [
            expert_ids.astype(jnp.bfloat16),
            jnp.broadcast_to(asks.reshape(1, -1), (token_rows, owner_count * CAPP)),
        ],
        axis=1,
    )
    extra = jnp.pad(extra, ((0, 0), (0, ASK_LANES - extra.shape[1])))
    gathered = gather_all(jnp.concatenate([tokens, extra], axis=1), dp_count, slice_count)

    me = lax.axis_index("expert")
    first = gathered[:, 0, features:].reshape(owner_count, dp_count, ASK_LANES)[:, 0]
    asked = first[:, top_count : top_count + owner_count * CAPP]
    asked = lax.dynamic_index_in_dim(
        asked.reshape(owner_count, owner_count, CAPP), me, axis=1, keepdims=False
    )

    mine = ((me * dp_count + lax.axis_index("dp")) // split_count).astype(jnp.bfloat16)
    routed = jnp.any(gathered[:, :, features : features + top_count] == mine, axis=2)
    rank_in = jnp.dot(
        routed.astype(jnp.bfloat16), before.T, preferred_element_type=jnp.float32
    ).astype(jnp.int32)
    place_in = jnp.arange(slice_count, dtype=jnp.int32)[:, None] * capacity + rank_in
    place_in = jnp.where(routed, place_in, -1).reshape(-1)
    dispatch = (
        jnp.arange(slice_count * capacity, dtype=jnp.int32)[:, None] == place_in[None, :]
    ).astype(jnp.bfloat16)
    lines = latent_pool.reshape(pool_rows, page_width // 128, 128)
    fetched = lines.at[asked.astype(jnp.int32)].get(mode="clip")
    arrived = lax.all_to_all(fetched, "expert", split_axis=0, concat_axis=0, tiled=True)

    received = jnp.dot(
        dispatch, gathered.reshape(slice_count * token_rows, -1), preferred_element_type=jnp.float32
    ).astype(jnp.bfloat16)
    parts = expert_mlp(received, w_gate, w_up, w_down)
    parts, arrived = lax.optimization_barrier((parts, arrived))
    returned = lax.all_to_all(
        parts.reshape(slice_count, capacity, features), both, split_axis=0, concat_axis=0, tiled=True
    )

    page_at = refs_owner * CAPP + ref_rank
    cached = (
        arrived.reshape(owner_count * CAPP, page_width // 128, 128)
        .at[page_at]
        .get(mode="clip")
        .reshape(request_count, page_count * page_rows, LAT)
    )
    keys = jnp.concatenate([cached, new_latent.reshape(request_count, -1, LAT)], axis=1)
    context = attend(queries, keys, prefix_len)

    summed = returned.reshape(EXPERTS, split_count, capacity, features)
    summed = jnp.sum(summed, axis=1, dtype=jnp.float32).reshape(EXPERTS * capacity, features)
    weight = jnp.sum(
        jnp.where(
            expert_ids[:, :, None] == jnp.arange(EXPERTS, dtype=jnp.int32)[None, None, :],
            gates[:, :, None],
            0.0,
        ),
        axis=1,
    )
    weighting = jnp.where(chosen, weight.T[:, None, :], 0.0).reshape(
        EXPERTS * capacity, token_rows
    )
    moe_out = lax.dot_general(
        weighting,
        summed,
        (((0,), (0,)), ((), ())),
        precision=lax.Precision.HIGHEST,
        preferred_element_type=jnp.float32,
    ).astype(jnp.bfloat16)
    return (context, moe_out)


def solution(mesh):
    return jax.shard_map(
        per_device,
        mesh=mesh,
        in_specs=(
            P(("groups", "expert"), None),
            P(("groups", "expert"), None),
            P(("groups", "expert"), None),
            P(("groups", "expert")),
            P(("groups", "expert"), None, "dp"),
            P(("groups", "expert"), None),
            P(("groups", "expert", "dp"), None),
            P(("groups", "expert", "dp"), None),
            P(("groups", "expert", "dp"), None),
            P(("expert", "dp"), None, None),
            P(("expert", "dp"), None, None),
            P(("expert", "dp"), None, None),
        ),
        out_specs=(P(("groups", "expert"), None, "dp"), P(("groups", "expert", "dp"), None)),
        check_vma=False,
    )
```

```python
import functools

import jax
import jax.numpy as jnp
from jax import lax
from jax.experimental import pallas as pl
from jax.experimental.pallas import tpu as pltpu
from jax.sharding import PartitionSpec as P

LATENT = 512
ROPE = 64
LAT = LATENT + ROPE
EXPERTS = 16
CAPP = 2
ASK_LANES = 128
CHUNK_ROWS = 16
WINDOW = 640
LOG2E = 1.4426950408889634
SCALE = 192.0 ** (-0.5)
VMEM_LIMIT = 48 * 1024 * 1024


def attend_kernel(length_ref, q_ref, even_ref, odd_ref, o_ref):
    length = length_ref[pl.program_id(0)]
    new_rows = q_ref.shape[1]
    pairs = q_ref.shape[2] // (2 * LAT)
    values = even_ref[0, :, :LATENT]
    for half, (key_ref, start) in enumerate(((even_ref, 0), (odd_ref, LATENT))):
        rows = jnp.concatenate(
            [q_ref[0, :, p * 2 * LAT + start : p * 2 * LAT + start + WINDOW] for p in range(pairs)],
            axis=0,
        )
        scores = lax.dot_general(
            rows, key_ref[0], (((1,), (1,)), ((), ())), preferred_element_type=jnp.float32
        )
        prefix_cap = scores.shape[1] - new_rows
        position = lax.broadcasted_iota(jnp.int32, scores.shape, 1)
        row = lax.rem(lax.broadcasted_iota(jnp.int32, scores.shape, 0), new_rows)
        visible = jnp.logical_or(
            position < length,
            jnp.logical_and(position >= prefix_cap, position - prefix_cap <= row),
        )
        scores = jnp.where(visible, scores, -1e30)
        highest = jnp.max(scores, axis=-1, keepdims=True)
        weights = jnp.exp2((scores - highest) * (SCALE * LOG2E))
        total = jnp.sum(weights, axis=-1, keepdims=True)
        probs = (weights * (1.0 / total)).astype(jnp.bfloat16)
        context = jnp.dot(probs, values, preferred_element_type=jnp.float32).astype(o_ref.dtype)
        for p in range(pairs):
            at = (2 * p + half) * LATENT
            o_ref[0, :, at : at + LATENT] = context[p * new_rows : (p + 1) * new_rows]


def attend(queries, keys, prefix_len):
    requests, new_rows, width = queries.shape
    heads = width // LAT
    block = 16 if heads % 16 == 0 else 2
    key_rows = keys.shape[1]
    even = jnp.pad(keys, ((0, 0), (0, 0), (0, WINDOW - LAT)))
    odd = jnp.pad(keys, ((0, 0), (0, 0), (WINDOW - LAT, 0)))
    key_spec = pl.BlockSpec((1, key_rows, WINDOW), lambda r, h, *_: (r, 0, 0))
    return pl.pallas_call(
        attend_kernel,
        out_shape=jax.ShapeDtypeStruct((requests, new_rows, heads * LATENT), jnp.bfloat16),
        grid_spec=pltpu.PrefetchScalarGridSpec(
            num_scalar_prefetch=1,
            grid=(requests, heads // block),
            in_specs=[
                pl.BlockSpec((1, new_rows, block * LAT), lambda r, h, *_: (r, 0, h)),
                key_spec,
                key_spec,
            ],
            out_specs=pl.BlockSpec((1, new_rows, block * LATENT), lambda r, h, *_: (r, 0, h)),
        ),
        compiler_params=pltpu.CompilerParams(vmem_limit_bytes=VMEM_LIMIT),
        cost_estimate=pl.CostEstimate(
            flops=2 * requests * new_rows * heads * key_rows * (LAT + LATENT),
            bytes_accessed=2 * requests * new_rows * heads * (LAT + LATENT),
            transcendentals=requests * new_rows * heads * key_rows,
        ),
    )(prefix_len, queries, even, odd)


def mlp_kernel(x_ref, gate_ref, up_ref, down_ref, o_ref, total):
    step = pl.program_id(0)
    x = x_ref[...]
    gate_val = jnp.dot(x, gate_ref[0], preferred_element_type=jnp.float32)
    upward = jnp.dot(x, up_ref[0], preferred_element_type=jnp.float32)
    hidden = (gate_val / (1.0 + jnp.exp(-gate_val)) * upward).astype(jnp.bfloat16)
    columns = 512
    for c in range(0, o_ref.shape[1], columns):
        product = jnp.dot(
            hidden, down_ref[0, :, c : c + columns], preferred_element_type=jnp.float32
        )

        @pl.when(step == 0)
        def _():
            total[:, c : c + columns] = product

        @pl.when(step > 0)
        def _():
            total[:, c : c + columns] += product

    @pl.when(step == pl.num_programs(0) - 1)
    def _():
        o_ref[...] = total[...].astype(o_ref.dtype)


def expert_mlp(x, w_gate, w_up, w_down):
    rows, features = x.shape[0], w_gate.shape[1]
    units = w_gate.shape[2]
    tile = min(256, units)
    whole = pl.BlockSpec((rows, features), lambda i: (0, 0), pipeline_mode=pl.Buffered(1))
    return pl.pallas_call(
        mlp_kernel,
        out_shape=jax.ShapeDtypeStruct((rows, features), jnp.bfloat16),
        grid=(units // tile,),
        in_specs=[
            whole,
            pl.BlockSpec((1, features, tile), lambda i: (0, 0, i)),
            pl.BlockSpec((1, features, tile), lambda i: (0, 0, i)),
            pl.BlockSpec((1, tile, features), lambda i: (0, i, 0)),
        ],
        out_specs=pl.BlockSpec((rows, features), lambda i: (0, 0)),
        scratch_shapes=[pltpu.VMEM((rows, features), jnp.float32)],
        compiler_params=pltpu.CompilerParams(vmem_limit_bytes=VMEM_LIMIT),
        cost_estimate=pl.CostEstimate(
            flops=6 * rows * features * units,
            bytes_accessed=6 * features * units + 4 * rows * features,
            transcendentals=rows * units,
        ),
    )(x, w_gate, w_up, w_down)


def gather_kernel(n, dp_count, own_ref, all_ref, local_sem, ring_out, ring_in, pair_out, pair_in):
    flat = lax.axis_index("expert") * dp_count + lax.axis_index("dp")
    group = lax.axis_index("groups")
    chip, core = lax.div(flat, 2), lax.rem(flat, 2)
    if dp_count == 1:
        column, level = lax.rem(chip, 2), lax.div(chip, 2)
        place = level + column * (n - 1 - 2 * level)
    else:
        place = chip

    def at(offset):
        q = lax.rem(place + offset + n, n)
        if dp_count == 1:
            down = lax.div(q, n // 2)
            q = 2 * (q + down * (n - 1 - 2 * q)) + down
        return 2 * q + core

    rows = CHUNK_ROWS
    chunks = own_ref.shape[0] // rows

    def piece(ref, chunk):
        return ref.at[pl.ds(chunk * rows, rows)]

    def copy(src, block, chunk, send, recv, target):
        return pltpu.make_async_remote_copy(
            src_ref=piece(src, chunk),
            dst_ref=piece(all_ref.at[block], chunk),
            send_sem=send,
            recv_sem=recv,
            device_id=(group, lax.div(target, dp_count), lax.rem(target, dp_count)),
            device_id_type=pl.DeviceIdType.MESH,
        )

    right, left, other = at(1), at(-1), flat + 1 - 2 * core
    barrier = pltpu.get_barrier_semaphore()
    for target in (right, left, other):
        pl.semaphore_signal(
            barrier,
            inc=1,
            device_id=(group, lax.div(target, dp_count), lax.rem(target, dp_count)),
            device_id_type=pl.DeviceIdType.MESH,
        )
    pl.semaphore_wait(barrier, 3)

    hops = [
        [n // 2 if way == chunk % 2 else n - 1 - n // 2 for way in (0, 1)]
        for chunk in range(chunks)
    ]
    ring, pair = {}, []

    def ring_start(chunk, way, hop, src, block):
        k = len(ring)
        ring[chunk, way, hop] = copy(
            src, block, chunk, ring_out.at[k], ring_in.at[k], (right, left)[way]
        )
        ring[chunk, way, hop].start()

    def pair_start(chunk, src, block):
        j = len(pair)
        pair.append(copy(src, block, chunk, pair_out.at[j], pair_in.at[j], other))
        pair[-1].start()

    for chunk in range(chunks):
        for way in (0, 1):
            ring_start(chunk, way, 0, own_ref, flat)
    local = pltpu.make_async_copy(own_ref, all_ref.at[flat], local_sem)
    local.start()
    for chunk in range(chunks):
        pair_start(chunk, own_ref, flat)
    for hop in range(n // 2):
        for chunk in range(chunks):
            for way in (0, 1):
                if hop < hops[chunk][way]:
                    block = at((-1, 1)[way] * (hop + 1))
                    ring[chunk, way, hop].wait_recv()
                    if hop + 1 < hops[chunk][way]:
                        ring_start(chunk, way, hop + 1, all_ref.at[block], block)
                    pair_start(chunk, all_ref.at[block], block)
    for sent in ring.values():
        sent.wait_send()
    for sent in pair:
        sent.wait()
    local.wait()


def gather_all(block, dp_count, count):
    n = count // 2
    chunks = block.shape[0] // CHUNK_ROWS
    return pl.pallas_call(
        functools.partial(gather_kernel, n, dp_count),
        out_shape=jax.ShapeDtypeStruct((count,) + block.shape, block.dtype),
        in_specs=[pl.BlockSpec(memory_space=pl.ANY)],
        out_specs=pl.BlockSpec(memory_space=pl.ANY),
        scratch_shapes=[
            pltpu.SemaphoreType.DMA,
            pltpu.SemaphoreType.DMA((chunks * (n - 1),)),
            pltpu.SemaphoreType.DMA((chunks * (n - 1),)),
            pltpu.SemaphoreType.DMA((chunks * n,)),
            pltpu.SemaphoreType.DMA((chunks * n,)),
        ],
        compiler_params=pltpu.CompilerParams(collective_id=0, has_side_effects=True),
    )(block)


def per_device(
    latent_pool,
    page_owner,
    page_slot,
    prefix_len,
    queries,
    new_latent,
    tokens,
    expert_ids,
    gates,
    w_gate,
    w_up,
    w_down,
):
    owner_count = lax.axis_size("expert")
    dp_count = lax.axis_size("dp")
    request_count, page_count = page_owner.shape
    pool_rows, page_width = latent_pool.shape
    page_rows = page_width // LAT
    token_rows, features = tokens.shape
    top_count = expert_ids.shape[1]
    capacity = 3 * token_rows * top_count // (2 * EXPERTS)
    slice_count = owner_count * dp_count
    split_count = slice_count // EXPERTS
    both = ("expert", "dp")

    wanted = jnp.any(
        expert_ids[:, :, None] == jnp.arange(EXPERTS, dtype=jnp.int32)[None, None, :], axis=1
    ).astype(jnp.bfloat16)
    before = (
        jnp.arange(token_rows)[:, None] > jnp.arange(token_rows)[None, :]
    ).astype(jnp.bfloat16)
    rank = jnp.dot(before, wanted, preferred_element_type=jnp.float32).astype(jnp.int32)
    place = jnp.where(
        wanted > 0, rank + capacity * jnp.arange(EXPERTS, dtype=jnp.int32)[None, :], -1
    )
    chosen = place.T[:, None, :] == jnp.arange(EXPERTS * capacity, dtype=jnp.int32).reshape(
        EXPERTS, capacity, 1
    )

    refs_owner = page_owner.reshape(-1)
    named = refs_owner[:, None] == jnp.arange(owner_count, dtype=jnp.int32)[None, :]
    ref_at = jnp.arange(refs_owner.shape[0], dtype=jnp.int32)
    same = (refs_owner[:, None] == refs_owner[None, :]) & (ref_at[None, :] < ref_at[:, None])
    ref_rank = jnp.sum(same.astype(jnp.int32), axis=1)
    asks = jnp.sum(
        jnp.where(
            named[:, :, None]
            & (ref_rank[:, None, None] == jnp.arange(CAPP, dtype=jnp.int32)[None, None, :]),
            page_slot.reshape(-1)[:, None, None],
            0,
        ),
        axis=0,
    ).astype(jnp.bfloat16)
    extra = jnp.concatenate(
        [
            expert_ids.astype(jnp.bfloat16),
            jnp.broadcast_to(asks.reshape(1, -1), (token_rows, owner_count * CAPP)),
        ],
        axis=1,
    )
    extra = jnp.pad(extra, ((0, 0), (0, ASK_LANES - extra.shape[1])))
    gathered = gather_all(jnp.concatenate([tokens, extra], axis=1), dp_count, slice_count)

    me = lax.axis_index("expert")
    first = gathered[:, 0, features:].reshape(owner_count, dp_count, ASK_LANES)[:, 0]
    asked = first[:, top_count : top_count + owner_count * CAPP]
    asked = lax.dynamic_index_in_dim(
        asked.reshape(owner_count, owner_count, CAPP), me, axis=1, keepdims=False
    )

    mine = ((me * dp_count + lax.axis_index("dp")) // split_count).astype(jnp.bfloat16)
    routed = jnp.any(gathered[:, :, features : features + top_count] == mine, axis=2)
    rank_in = jnp.dot(
        routed.astype(jnp.bfloat16), before.T, preferred_element_type=jnp.float32
    ).astype(jnp.int32)
    place_in = jnp.arange(slice_count, dtype=jnp.int32)[:, None] * capacity + rank_in
    place_in = jnp.where(routed, place_in, -1).reshape(-1)
    dispatch = (
        jnp.arange(slice_count * capacity, dtype=jnp.int32)[:, None] == place_in[None, :]
    ).astype(jnp.bfloat16)
    lines = latent_pool.reshape(pool_rows, page_width // 128, 128)
    fetched = lines.at[asked.astype(jnp.int32)].get(mode="clip")
    arrived = lax.all_to_all(fetched, "expert", split_axis=0, concat_axis=0, tiled=True)

    received = jnp.dot(
        dispatch, gathered.reshape(slice_count * token_rows, -1), preferred_element_type=jnp.float32
    ).astype(jnp.bfloat16)
    parts = expert_mlp(received, w_gate, w_up, w_down)
    parts, arrived = lax.optimization_barrier((parts, arrived))
    returned = lax.all_to_all(
        parts.reshape(slice_count, capacity, features), both, split_axis=0, concat_axis=0, tiled=True
    )

    page_at = refs_owner * CAPP + ref_rank
    cached = (
        arrived.reshape(owner_count * CAPP, page_width // 128, 128)
        .at[page_at]
        .get(mode="clip")
        .reshape(request_count, page_count * page_rows, LAT)
    )
    keys = jnp.concatenate([cached, new_latent.reshape(request_count, -1, LAT)], axis=1)
    context = attend(queries, keys, prefix_len)

    summed = returned.reshape(EXPERTS, split_count, capacity, features)
    summed = jnp.sum(summed, axis=1, dtype=jnp.float32).reshape(EXPERTS * capacity, features)
    weight = jnp.sum(
        jnp.where(
            expert_ids[:, :, None] == jnp.arange(EXPERTS, dtype=jnp.int32)[None, None, :],
            gates[:, :, None],
            0.0,
        ),
        axis=1,
    )
    weighting = jnp.where(chosen, weight.T[:, None, :], 0.0).reshape(
        EXPERTS * capacity, token_rows
    )
    moe_out = lax.dot_general(
        weighting,
        summed,
        (((0,), (0,)), ((), ())),
        precision=lax.Precision.HIGHEST,
        preferred_element_type=jnp.float32,
    ).astype(jnp.bfloat16)
    return (context, moe_out)


def solution(mesh):
    return jax.shard_map(
        per_device,
        mesh=mesh,
        in_specs=(
            P(("groups", "expert"), None),
            P(("groups", "expert"), None),
            P(("groups", "expert"), None),
            P(("groups", "expert")),
            P(("groups", "expert"), None, "dp"),
            P(("groups", "expert"), None),
            P(("groups", "expert", "dp"), None),
            P(("groups", "expert", "dp"), None),
            P(("groups", "expert", "dp"), None),
            P(("expert", "dp"), None, None),
            P(("expert", "dp"), None, None),
            P(("expert", "dp"), None, None),
        ),
        out_specs=(P(("groups", "expert"), None, "dp"), P(("groups", "expert", "dp"), None)),
        check_vma=False,
    )
```

```python
import functools

import jax
import jax.numpy as jnp
from jax import lax
from jax.experimental import pallas as pl
from jax.experimental.pallas import tpu as pltpu
from jax.sharding import PartitionSpec as P

LATENT = 512
ROPE = 64
LAT = LATENT + ROPE
EXPERTS = 16
CAPP = 2
ASK_LANES = 128
CHUNK_ROWS = 16
WINDOW = 640
LOG2E = 1.4426950408889634
SCALE = 192.0 ** (-0.5)
VMEM_LIMIT = 48 * 1024 * 1024


def attend_kernel(length_ref, q_ref, even_ref, odd_ref, o_ref):
    length = length_ref[pl.program_id(0)]
    new_rows = q_ref.shape[1]
    pairs = q_ref.shape[2] // (2 * LAT)
    values = even_ref[0, :, :LATENT]
    for half, (key_ref, start) in enumerate(((even_ref, 0), (odd_ref, LATENT))):
        rows = jnp.concatenate(
            [q_ref[0, :, p * 2 * LAT + start : p * 2 * LAT + start + WINDOW] for p in range(pairs)],
            axis=0,
        )
        scores = lax.dot_general(
            rows, key_ref[0], (((1,), (1,)), ((), ())), preferred_element_type=jnp.float32
        )
        prefix_cap = scores.shape[1] - new_rows
        position = lax.broadcasted_iota(jnp.int32, scores.shape, 1)
        row = lax.rem(lax.broadcasted_iota(jnp.int32, scores.shape, 0), new_rows)
        visible = jnp.logical_or(
            position < length,
            jnp.logical_and(position >= prefix_cap, position - prefix_cap <= row),
        )
        scores = jnp.where(visible, scores, -1e30)
        highest = jnp.max(scores, axis=-1, keepdims=True)
        weights = jnp.exp2((scores - highest) * (SCALE * LOG2E))
        total = jnp.sum(weights, axis=-1, keepdims=True)
        probs = (weights * (1.0 / total)).astype(jnp.bfloat16)
        context = jnp.dot(probs, values, preferred_element_type=jnp.float32).astype(o_ref.dtype)
        for p in range(pairs):
            at = (2 * p + half) * LATENT
            o_ref[0, :, at : at + LATENT] = context[p * new_rows : (p + 1) * new_rows]


def attend(queries, keys, prefix_len):
    requests, new_rows, width = queries.shape
    heads = width // LAT
    block = 16 if heads % 16 == 0 else 2
    key_rows = keys.shape[1]
    even = jnp.pad(keys, ((0, 0), (0, 0), (0, WINDOW - LAT)))
    odd = jnp.pad(keys, ((0, 0), (0, 0), (WINDOW - LAT, 0)))
    key_spec = pl.BlockSpec((1, key_rows, WINDOW), lambda r, h, *_: (r, 0, 0))
    return pl.pallas_call(
        attend_kernel,
        out_shape=jax.ShapeDtypeStruct((requests, new_rows, heads * LATENT), jnp.bfloat16),
        grid_spec=pltpu.PrefetchScalarGridSpec(
            num_scalar_prefetch=1,
            grid=(requests, heads // block),
            in_specs=[
                pl.BlockSpec((1, new_rows, block * LAT), lambda r, h, *_: (r, 0, h)),
                key_spec,
                key_spec,
            ],
            out_specs=pl.BlockSpec((1, new_rows, block * LATENT), lambda r, h, *_: (r, 0, h)),
        ),
        compiler_params=pltpu.CompilerParams(vmem_limit_bytes=VMEM_LIMIT),
        cost_estimate=pl.CostEstimate(
            flops=2 * requests * new_rows * heads * key_rows * (LAT + LATENT),
            bytes_accessed=2 * requests * new_rows * heads * (LAT + LATENT),
            transcendentals=requests * new_rows * heads * key_rows,
        ),
    )(prefix_len, queries, even, odd)


def mlp_kernel(x_ref, gate_ref, up_ref, down_ref, o_ref, total):
    step = pl.program_id(0)
    x = x_ref[...]
    gate_val = jnp.dot(x, gate_ref[0], preferred_element_type=jnp.float32)
    upward = jnp.dot(x, up_ref[0], preferred_element_type=jnp.float32)
    hidden = (gate_val / (1.0 + jnp.exp(-gate_val)) * upward).astype(jnp.bfloat16)
    columns = 512
    for c in range(0, o_ref.shape[1], columns):
        product = jnp.dot(
            hidden, down_ref[0, :, c : c + columns], preferred_element_type=jnp.float32
        )

        @pl.when(step == 0)
        def _():
            total[:, c : c + columns] = product

        @pl.when(step > 0)
        def _():
            total[:, c : c + columns] += product

    @pl.when(step == pl.num_programs(0) - 1)
    def _():
        o_ref[...] = total[...].astype(o_ref.dtype)


def expert_mlp(x, w_gate, w_up, w_down):
    rows, features = x.shape[0], w_gate.shape[1]
    units = w_gate.shape[2]
    tile = min(256, units)
    whole = pl.BlockSpec((rows, features), lambda i: (0, 0), pipeline_mode=pl.Buffered(1))
    return pl.pallas_call(
        mlp_kernel,
        out_shape=jax.ShapeDtypeStruct((rows, features), jnp.bfloat16),
        grid=(units // tile,),
        in_specs=[
            whole,
            pl.BlockSpec((1, features, tile), lambda i: (0, 0, i)),
            pl.BlockSpec((1, features, tile), lambda i: (0, 0, i)),
            pl.BlockSpec((1, tile, features), lambda i: (0, i, 0)),
        ],
        out_specs=pl.BlockSpec((rows, features), lambda i: (0, 0)),
        scratch_shapes=[pltpu.VMEM((rows, features), jnp.float32)],
        compiler_params=pltpu.CompilerParams(vmem_limit_bytes=VMEM_LIMIT),
        cost_estimate=pl.CostEstimate(
            flops=6 * rows * features * units,
            bytes_accessed=6 * features * units + 4 * rows * features,
            transcendentals=rows * units,
        ),
    )(x, w_gate, w_up, w_down)


def gather_kernel(n, dp_count, own_ref, all_ref, local_sem, ring_out, ring_in, pair_out, pair_in):
    flat = lax.axis_index("expert") * dp_count + lax.axis_index("dp")
    group = lax.axis_index("groups")
    chip, core = lax.div(flat, 2), lax.rem(flat, 2)
    if dp_count == 1:
        column, level = lax.rem(chip, 2), lax.div(chip, 2)
        place = level + column * (n - 1 - 2 * level)
    else:
        place = chip

    def at(offset):
        q = lax.rem(place + offset + n, n)
        if dp_count == 1:
            down = lax.div(q, n // 2)
            q = 2 * (q + down * (n - 1 - 2 * q)) + down
        return 2 * q + core

    rows = CHUNK_ROWS
    chunks = own_ref.shape[0] // rows

    def piece(ref, chunk):
        return ref.at[pl.ds(chunk * rows, rows)]

    def copy(src, block, chunk, send, recv, target):
        return pltpu.make_async_remote_copy(
            src_ref=piece(src, chunk),
            dst_ref=piece(all_ref.at[block], chunk),
            send_sem=send,
            recv_sem=recv,
            device_id=(group, lax.div(target, dp_count), lax.rem(target, dp_count)),
            device_id_type=pl.DeviceIdType.MESH,
        )

    right, left, other = at(1), at(-1), flat + 1 - 2 * core
    barrier = pltpu.get_barrier_semaphore()
    for target in (right, left, other):
        pl.semaphore_signal(
            barrier,
            inc=1,
            device_id=(group, lax.div(target, dp_count), lax.rem(target, dp_count)),
            device_id_type=pl.DeviceIdType.MESH,
        )
    pl.semaphore_wait(barrier, 3)

    hops = [
        [n // 2 if way == chunk % 2 else n - 1 - n // 2 for way in (0, 1)]
        for chunk in range(chunks)
    ]
    ring, pair = {}, []

    def ring_start(chunk, way, hop, src, block):
        k = len(ring)
        ring[chunk, way, hop] = copy(
            src, block, chunk, ring_out.at[k], ring_in.at[k], (right, left)[way]
        )
        ring[chunk, way, hop].start()

    def pair_start(chunk, src, block):
        j = len(pair)
        pair.append(copy(src, block, chunk, pair_out.at[j], pair_in.at[j], other))
        pair[-1].start()

    for chunk in range(chunks):
        for way in (0, 1):
            ring_start(chunk, way, 0, own_ref, flat)
    local = pltpu.make_async_copy(own_ref, all_ref.at[flat], local_sem)
    local.start()
    for chunk in range(chunks):
        pair_start(chunk, own_ref, flat)
    for hop in range(n // 2):
        for chunk in range(chunks):
            for way in (0, 1):
                if hop < hops[chunk][way]:
                    block = at((-1, 1)[way] * (hop + 1))
                    ring[chunk, way, hop].wait_recv()
                    if hop + 1 < hops[chunk][way]:
                        ring_start(chunk, way, hop + 1, all_ref.at[block], block)
                    pair_start(chunk, all_ref.at[block], block)
    for sent in ring.values():
        sent.wait_send()
    for sent in pair:
        sent.wait()
    local.wait()


def gather_all(block, dp_count, count):
    n = count // 2
    chunks = block.shape[0] // CHUNK_ROWS
    return pl.pallas_call(
        functools.partial(gather_kernel, n, dp_count),
        out_shape=jax.ShapeDtypeStruct((count,) + block.shape, block.dtype),
        in_specs=[pl.BlockSpec(memory_space=pl.ANY)],
        out_specs=pl.BlockSpec(memory_space=pl.ANY),
        scratch_shapes=[
            pltpu.SemaphoreType.DMA,
            pltpu.SemaphoreType.DMA((chunks * (n - 1),)),
            pltpu.SemaphoreType.DMA((chunks * (n - 1),)),
            pltpu.SemaphoreType.DMA((chunks * n,)),
            pltpu.SemaphoreType.DMA((chunks * n,)),
        ],
        compiler_params=pltpu.CompilerParams(collective_id=0, has_side_effects=True),
    )(block)


def per_device(
    latent_pool,
    page_owner,
    page_slot,
    prefix_len,
    queries,
    new_latent,
    tokens,
    expert_ids,
    gates,
    w_gate,
    w_up,
    w_down,
):
    owner_count = lax.axis_size("expert")
    dp_count = lax.axis_size("dp")
    request_count, page_count = page_owner.shape
    pool_rows, page_width = latent_pool.shape
    page_rows = page_width // LAT
    token_rows, features = tokens.shape
    top_count = expert_ids.shape[1]
    capacity = 3 * token_rows * top_count // (2 * EXPERTS)
    slice_count = owner_count * dp_count
    split_count = slice_count // EXPERTS
    both = ("expert", "dp")

    wanted = jnp.any(
        expert_ids[:, :, None] == jnp.arange(EXPERTS, dtype=jnp.int32)[None, None, :], axis=1
    ).astype(jnp.bfloat16)
    before = (
        jnp.arange(token_rows)[:, None] > jnp.arange(token_rows)[None, :]
    ).astype(jnp.bfloat16)
    rank = jnp.dot(before, wanted, preferred_element_type=jnp.float32).astype(jnp.int32)
    place = jnp.where(
        wanted > 0, rank + capacity * jnp.arange(EXPERTS, dtype=jnp.int32)[None, :], -1
    )
    chosen = place.T[:, None, :] == jnp.arange(EXPERTS * capacity, dtype=jnp.int32).reshape(
        EXPERTS, capacity, 1
    )

    refs_owner = page_owner.reshape(-1)
    named = refs_owner[:, None] == jnp.arange(owner_count, dtype=jnp.int32)[None, :]
    ref_at = jnp.arange(refs_owner.shape[0], dtype=jnp.int32)
    same = (refs_owner[:, None] == refs_owner[None, :]) & (ref_at[None, :] < ref_at[:, None])
    ref_rank = jnp.sum(same.astype(jnp.int32), axis=1)
    asks = jnp.sum(
        jnp.where(
            named[:, :, None]
            & (ref_rank[:, None, None] == jnp.arange(CAPP, dtype=jnp.int32)[None, None, :]),
            page_slot.reshape(-1)[:, None, None],
            0,
        ),
        axis=0,
    ).astype(jnp.bfloat16)
    extra = jnp.concatenate(
        [
            expert_ids.astype(jnp.bfloat16),
            jnp.broadcast_to(asks.reshape(1, -1), (token_rows, owner_count * CAPP)),
        ],
        axis=1,
    )
    extra = jnp.pad(extra, ((0, 0), (0, ASK_LANES - extra.shape[1])))
    gathered = gather_all(jnp.concatenate([tokens, extra], axis=1), dp_count, slice_count)

    me = lax.axis_index("expert")
    first = gathered[:, 0, features:].reshape(owner_count, dp_count, ASK_LANES)[:, 0]
    asked = first[:, top_count : top_count + owner_count * CAPP]
    asked = lax.dynamic_index_in_dim(
        asked.reshape(owner_count, owner_count, CAPP), me, axis=1, keepdims=False
    )

    mine = ((me * dp_count + lax.axis_index("dp")) // split_count).astype(jnp.bfloat16)
    routed = jnp.any(gathered[:, :, features : features + top_count] == mine, axis=2)
    rank_in = jnp.dot(
        routed.astype(jnp.bfloat16), before.T, preferred_element_type=jnp.float32
    ).astype(jnp.int32)
    place_in = jnp.arange(slice_count, dtype=jnp.int32)[:, None] * capacity + rank_in
    place_in = jnp.where(routed, place_in, -1).reshape(-1)
    dispatch = (
        jnp.arange(slice_count * capacity, dtype=jnp.int32)[:, None] == place_in[None, :]
    ).astype(jnp.bfloat16)
    lines = latent_pool.reshape(pool_rows, page_width // 128, 128)
    fetched = lines.at[asked.astype(jnp.int32)].get(mode="clip")
    arrived = lax.all_to_all(fetched, "expert", split_axis=0, concat_axis=0, tiled=True)

    received = jnp.dot(
        dispatch, gathered.reshape(slice_count * token_rows, -1), preferred_element_type=jnp.float32
    ).astype(jnp.bfloat16)
    parts = expert_mlp(received, w_gate, w_up, w_down)
    returned = lax.all_to_all(
        parts.reshape(slice_count, capacity, features), both, split_axis=0, concat_axis=0, tiled=True
    )

    page_at = refs_owner * CAPP + ref_rank
    cached = (
        arrived.reshape(owner_count * CAPP, page_width // 128, 128)
        .at[page_at]
        .get(mode="clip")
        .reshape(request_count, page_count * page_rows, LAT)
    )
    keys = jnp.concatenate([cached, new_latent.reshape(request_count, -1, LAT)], axis=1)
    context = attend(queries, keys, prefix_len)

    summed = returned.reshape(EXPERTS, split_count, capacity, features)
    summed = jnp.sum(summed, axis=1, dtype=jnp.float32).reshape(EXPERTS * capacity, features)
    weight = jnp.sum(
        jnp.where(
            expert_ids[:, :, None] == jnp.arange(EXPERTS, dtype=jnp.int32)[None, None, :],
            gates[:, :, None],
            0.0,
        ),
        axis=1,
    )
    weighting = jnp.where(chosen, weight.T[:, None, :], 0.0).reshape(
        EXPERTS * capacity, token_rows
    )
    moe_out = lax.dot_general(
        weighting,
        summed,
        (((0,), (0,)), ((), ())),
        precision=lax.Precision.HIGHEST,
        preferred_element_type=jnp.float32,
    ).astype(jnp.bfloat16)
    return (context, moe_out)


def solution(mesh):
    return jax.shard_map(
        per_device,
        mesh=mesh,
        in_specs=(
            P(("groups", "expert"), None),
            P(("groups", "expert"), None),
            P(("groups", "expert"), None),
            P(("groups", "expert")),
            P(("groups", "expert"), None, "dp"),
            P(("groups", "expert"), None),
            P(("groups", "expert", "dp"), None),
            P(("groups", "expert", "dp"), None),
            P(("groups", "expert", "dp"), None),
            P(("expert", "dp"), None, None),
            P(("expert", "dp"), None, None),
            P(("expert", "dp"), None, None),
        ),
        out_specs=(P(("groups", "expert"), None, "dp"), P(("groups", "expert", "dp"), None)),
        check_vma=False,
    )
```
